32 devices in a mesh: chan: 8 (over y, x, core), tm: 4 (over z).
Axes of the slice: x: 2, y: 2, z: 4, core: 2. Of those that a mesh axis runs over, the one named last changes fastest.
Arguments:
- records: bfloat16 [128, 16384], P('chan', 'tm'), may hold values from -100 to 100, as said below
- pair_rows: int32 [8, 16], P('chan'), may hold values from 0 to 15, each once within a row
- fir_taps: float32 [32], replicated, may hold values from -1 to 1
- source_blocks: int32 [2], replicated, may hold values from 0 to 15
Outputs:
- stacks: float32 [2, 8, 128, 1024], P(None, None, 'chan', 'tm')
The draws below stay inside these ranges and needn't reach their ends.
Inputs may be any that keep to these rules, and one draw needn't show every extreme that they name: Seismic noise records, one row a channel.
All inputs are finite; a program needn't handle non-finite values.
Results may differ from the reference program's by a relative error of at most 0.0037.
Values may be sent and summed in bfloat16 or wider, within the bound.
A program may use at most 128 MiB of HBM per device.

```python
import math
import jax
import jax.numpy as jnp
from jax import lax

CR = 16
VS = 8
STEPS = 2
LAGS = 1024
TAPS = 32
CHANNELS = 128
WINDOW = 4096
SAMPLES = 16384
SRC_BLOCKS = 16
N_CHAN = 8


def draw_records(key, part):
    key_scale, key_noise = jax.random.split(key, 2)
    row_scale = jnp.exp(jax.random.uniform(key_scale, (CHANNELS, 1), minval=0.0, maxval=math.log(10.0)))
    envelope = 1.0 + 0.8 * jnp.arange(SAMPLES, dtype=jnp.float32)[None, :] / SAMPLES
    noise = jnp.clip(jax.random.normal(key_noise, (CHANNELS, SAMPLES)), -5.0, 5.0)
    return (noise * row_scale * envelope).astype(jnp.bfloat16)


def scatter_about(key, shape, deviation, bound, held_as=jnp.bfloat16):
    values = jax.random.normal(key, shape, jnp.float32) * deviation
    return jnp.minimum(jnp.maximum(values, -bound), bound).astype(held_as)


def setup_inputs(seed: int = 0) -> dict:
    splits = jax.random.split(jax.random.key(seed), 5)
    records = draw_records(jax.random.fold_in(splits[4], 71), 0)
    pair_rows = jax.vmap(lambda own: jax.random.permutation(own, CR))(jax.random.split(splits[1], N_CHAN)).reshape((N_CHAN, CR)).astype(jnp.int32)
    fir_taps = scatter_about(splits[2], (TAPS,), TAPS ** -0.5, 1.0, jnp.float32)
    source_blocks = jax.random.randint(splits[3], (STEPS,), 0, SRC_BLOCKS).astype(jnp.int32)
    return {"records": records, "pair_rows": pair_rows, "fir_taps": fir_taps, "source_blocks": source_blocks}


def reference(records, pair_rows, fir_taps, source_blocks):
    blocks = records.reshape(N_CHAN, CR, SAMPLES)
    partner_block = (jnp.arange(N_CHAN) + N_CHAN // 2) % N_CHAN
    partner = blocks[partner_block]
    partner = jax.vmap(lambda block_rows, chosen: block_rows[chosen])(partner, pair_rows)
    combined = 0.5 * (records.astype(jnp.float32) + partner.reshape(CHANNELS, SAMPLES).astype(jnp.float32))
    padded = jnp.pad(combined, ((0, 0), (TAPS, 0)))
    filtered = jnp.zeros((CHANNELS, WINDOW), jnp.float32)
    for offset in range(TAPS):
        begin = TAPS + 3 - offset
        filtered = filtered + fir_taps[offset] * padded[:, begin:begin + 4 * WINDOW:4]
    power = lax.optimization_barrier(jnp.sum(filtered * filtered, axis=1)) / WINDOW
    whitened = (filtered * lax.rsqrt(power + 1e-06)[:, None]).astype(jnp.bfloat16)
    picked = []
    for step_index in range(STEPS):
        start_row = (source_blocks[step_index] * VS).astype(jnp.int32)
        picked.append(lax.dynamic_slice_in_dim(whitened, start_row, VS, 0))
    sources = jnp.stack(picked)
    fft_length = 2 * WINDOW
    spectra = jnp.fft.rfft(whitened.astype(jnp.float32), n=fft_length, axis=1)

    def one_source(source_row):
        source_spec = jnp.fft.rfft(source_row.astype(jnp.float32), n=fft_length)
        full_corr = jnp.fft.irfft(jnp.conj(source_spec)[None, :] * spectra, n=fft_length, axis=1)
        return full_corr[:, :LAGS]
    source_rows = sources.reshape(STEPS * VS, WINDOW)
    correlations = lax.map(one_source, source_rows)
    return (correlations.reshape(STEPS, VS, CHANNELS, LAGS) * (1.0 / math.sqrt(WINDOW))).astype(jnp.float32)
```

```python
import functools
import math

import jax
import jax.numpy as jnp
from jax import lax
from jax.experimental import pallas as pl
from jax.experimental.pallas import tpu as pltpu
from jax.sharding import PartitionSpec as P

VS = 8
STEPS = 2
LAGS = 1024
TAPS = 32
LANES = 128
FINE = 16


def body(C, T, rows, taps_ref, pair_ref, blocks_ref, rec_ref, out_ref,
         halo, filt, pfilt, pw, chw, tw, ts, sp, wp,
         halo_s, halo_r, part_s, part_r, pw_s, pw_r, ch_s, ch_r, tw_s, tw_r, ts_s, ts_r):
    me = lax.axis_index("chan")
    t = lax.axis_index("tm")
    f32, bf16 = jnp.float32, jnp.bfloat16
    samples = rec_ref.shape[1] // 4
    lag_dev = LAGS // T
    P_ = max(1, lag_dev // LANES)
    A_ = min(lag_dev, LANES) // FINE
    window = samples * T

    def at_chan(d):
        return lax.rem(me + d, C)

    def at_tm(d):
        return lax.rem(t + d, T)

    barrier = pltpu.get_barrier_semaphore()
    for d in range(1, C):
        pl.semaphore_signal(barrier, inc=1, device_id={"chan": at_chan(d)}, device_id_type=pl.DeviceIdType.MESH)
    for d in range(1, T):
        pl.semaphore_signal(barrier, inc=1, device_id={"tm": at_tm(d)}, device_id_type=pl.DeviceIdType.MESH)

    def remote(src, dst, ssem, rsem, where):
        return pltpu.make_async_remote_copy(
            src_ref=src, dst_ref=dst, send_sem=ssem, recv_sem=rsem,
            device_id=where, device_id_type=pl.DeviceIdType.MESH)

    group = 4 * LANES
    depth = LANES + group
    j = lax.broadcasted_iota(jnp.int32, (depth, LANES), 0)
    n = lax.broadcasted_iota(jnp.int32, (depth, LANES), 1)
    tap = 4 * n + 3 - (j - LANES)
    band = jnp.zeros((depth, LANES), f32)
    for k in range(TAPS):
        band = jnp.where(tap == k, taps_ref[k], band)
    hi = band.astype(bf16)
    lo = (band - hi.astype(f32)).astype(bf16)
    band2 = jnp.concatenate([hi, lo], axis=1)

    pl.semaphore_wait(barrier, C + T - 2)
    tail = rec_ref.shape[1] - LANES
    halo_copy = remote(rec_ref.at[:, pl.ds(tail, LANES)], halo, halo_s, halo_r, {"tm": at_tm(1)})
    halo_copy.start()

    sp[:, :LANES] = jnp.zeros((rows, LANES), f32)
    wp[:, window:] = jnp.zeros((rows, wp.shape[1] - window), f32)

    groups = samples // LANES
    parts = []
    for g in range(groups):
        if g == 0:
            first = jnp.zeros((rows, LANES), bf16)
        else:
            first = rec_ref[:, group * g - LANES:group * g]
        parts.append(jnp.concatenate([first, rec_ref[:, group * g:group * (g + 1)]], axis=1))
    lhs = jnp.concatenate(parts, axis=0)
    both = jnp.dot(lhs, band2, preferred_element_type=f32)
    res = both[:, :LANES] + both[:, LANES:]
    halo_copy.wait()
    edge = jnp.dot(halo[...], band2[:LANES], preferred_element_type=f32)
    edge = edge[:, :LANES] + edge[:, LANES:]
    edge = jnp.where(t > 0, edge, jnp.zeros_like(edge))
    for g in range(groups):
        piece = res[rows * g:rows * (g + 1)]
        if g == 0:
            piece = piece + edge
        filt[:, LANES * g:LANES * (g + 1)] = piece
    part_copy = remote(filt, pfilt, part_s, part_r, {"chan": at_chan(C // 2)})
    part_copy.start()
    rr = lax.broadcasted_iota(jnp.int32, (rows, rows), 0)
    cc = lax.broadcasted_iota(jnp.int32, (rows, rows), 1)
    pick = jnp.zeros((rows, rows), jnp.int32)
    for r in range(rows):
        pick = jnp.where(rr == r, pair_ref[0, r], pick)
    perm = jnp.where(pick == cc, 1.0, 0.0).astype(f32)
    part_copy.wait()
    filtered = 0.5 * (filt[...] + jnp.dot(perm, pfilt[...], precision=lax.Precision.HIGHEST,
                                          preferred_element_type=f32))
    sq = filtered * filtered
    acc = sq[:, :LANES]
    for g in range(1, groups):
        acc = acc + sq[:, LANES * g:LANES * (g + 1)]
    pw[t] = acc

    def spread(buf, slot, ssem, rsem, count, axis, place):
        sends = [remote(buf.at[slot], buf.at[slot], ssem.at[d], rsem.at[d], {axis: place(d)})
                 for d in range(1, count)]
        for s in sends:
            s.start()
        return sends

    def arrive(buf, ssem, rsem, count, axis, place):
        for d in range(1, count):
            slot = place(count - d)
            remote(buf.at[slot], buf.at[slot], ssem.at[d], rsem.at[d], {axis: place(d)}).wait_recv()

    pw_sends = spread(pw, t, pw_s, pw_r, T, "tm", at_tm)
    arrive(pw, pw_s, pw_r, T, "tm", at_tm)
    total = pw[0]
    for i in range(1, T):
        total = total + pw[i]
    power = jnp.sum(total, axis=1, keepdims=True) / window
    white = (filtered * lax.rsqrt(power + 1e-6)).astype(bf16)
    chw[me] = white
    tw[t] = white
    ch_sends = spread(chw, me, ch_s, ch_r, C, "chan", at_chan)
    tw_sends = spread(tw, t, tw_s, tw_r, T, "tm", at_tm)

    arrive(chw, ch_s, ch_r, C, "chan", at_chan)
    picked = []
    per = rows // VS
    for step in range(STEPS):
        blk = blocks_ref[step]
        owner = lax.div(blk, per)
        within = lax.rem(blk, per)
        x = chw[owner].astype(f32)
        half = x[:VS]
        for q in range(1, per):
            half = jnp.where(within == q, x[VS * q:VS * (q + 1)], half)
        picked.append(half)
    ts[t] = jnp.concatenate(picked, axis=0).astype(bf16)
    ts_sends = spread(ts, t, ts_s, ts_r, T, "tm", at_tm)
    arrive(tw, tw_s, tw_r, T, "tm", at_tm)
    for i in range(T):
        wp[:, samples * i:samples * (i + 1)] = tw[i].astype(f32)
    arrive(ts, ts_s, ts_r, T, "tm", at_tm)
    for i in range(T):
        sp[:, LANES + samples * i:LANES + samples * (i + 1)] = ts[i].astype(f32)

    lag0 = t * lag_dev
    wide = samples + LANES * P_
    if lag_dev % LANES == 0:
        base, rest = lag0, 0
    else:
        base = lax.div(lag0, LANES) * LANES
        rest = lax.rem(lag0, LANES)

    def block(i, z):
        s0 = pl.multiple_of(i * samples, LANES)
        w0 = pl.multiple_of(i * samples + base, LANES)
        srows = sp[:, pl.ds(s0, samples + LANES)]
        wrows = wp[:, pl.ds(w0, wide)]
        xs = []
        for s in range(STEPS * VS):
            one = jnp.broadcast_to(srows[s:s + 1], (FINE, samples + LANES))
            xs.append(pltpu.roll(one, 0, 1, stride=1, stride_axis=0)[:, LANES:].astype(bf16))
        rolled = []
        for a in range(A_):
            if lag_dev % LANES == 0:
                sh = (wide - FINE * a) % wide
            else:
                sh = wide - FINE * a - rest
            rolled.append(pltpu.roll(wrows, sh, 1) if not (isinstance(sh, int) and sh == 0) else wrows)
        ws = [rolled[a][:, LANES * p:LANES * p + samples].astype(bf16)
              for p in range(P_) for a in range(A_)]
        return z + lax.dot_general(jnp.concatenate(ws, axis=0), jnp.concatenate(xs, axis=0),
                                   (((1,), (1,)), ((), ())), preferred_element_type=f32)

    z = lax.fori_loop(0, T, block, jnp.zeros((P_ * A_ * rows, STEPS * VS * FINE), f32))
    z = z * (1.0 / math.sqrt(window))

    lane_group = lax.broadcasted_iota(jnp.int32, (rows, LANES), 1) // FINE
    per_tile = LANES // FINE
    width = min(lag_dev, LANES)
    for p in range(P_):
        for s in range(STEPS * VS):
            lo_s = s // per_tile * LANES
            o = None
            for a in range(A_):
                r0 = (p * A_ + a) * rows
                tile = z[r0:r0 + rows, lo_s:lo_s + LANES]
                sh = (FINE * (a - s % per_tile)) % LANES
                if sh:
                    tile = pltpu.roll(tile, sh, 1)
                o = tile if o is None else jnp.where(lane_group == a, tile, o)
            out_ref[s, :, LANES * p:LANES * p + width] = o[:, :width]

    for s in pw_sends + ch_sends + tw_sends + ts_sends:
        s.wait_send()


def shards(records, pair_rows, fir_taps, source_blocks):
    C = lax.axis_size("chan")
    T = lax.axis_size("tm")
    rows, raw = records.shape
    samples = raw // 4
    f32, bf16 = jnp.float32, jnp.bfloat16
    dma = pltpu.SemaphoreType.DMA
    vmem = pl.BlockSpec(memory_space=pltpu.VMEM)
    smem = pl.BlockSpec(memory_space=pltpu.SMEM)
    out = pl.pallas_call(
        functools.partial(body, C, T, rows),
        out_shape=jax.ShapeDtypeStruct((STEPS * VS, rows, LAGS // T), f32),
        in_specs=[smem, smem, smem, vmem],
        out_specs=vmem,
        scratch_shapes=[
            pltpu.VMEM((rows, LANES), bf16),
            pltpu.VMEM((rows, samples), f32),
            pltpu.VMEM((rows, samples), f32),
            pltpu.VMEM((T, rows, LANES), f32),
            pltpu.VMEM((C, rows, samples), bf16),
            pltpu.VMEM((T, rows, samples), bf16),
            pltpu.VMEM((T, rows, samples), bf16),
            pltpu.VMEM((rows, LANES + T * samples), f32),
            pltpu.VMEM((rows, T * samples + LAGS + LANES), f32),
            dma, dma, dma, dma,
            dma((T,)), dma((T,)), dma((C,)), dma((C,)),
            dma((T,)), dma((T,)), dma((T,)), dma((T,)),
        ],
        compiler_params=pltpu.CompilerParams(
            collective_id=0, has_side_effects=True, vmem_limit_bytes=32 * 2**20),
        cost_estimate=pl.CostEstimate(flops=600_000_000, bytes_accessed=1_000_000, transcendentals=0),
    )(fir_taps, pair_rows, source_blocks, records)
    return out.reshape(STEPS, VS, rows, LAGS // T)


def solution(mesh):
    return jax.shard_map(
        shards,
        mesh=mesh,
        in_specs=(P("chan", "tm"), P("chan", None), P(), P()),
        out_specs=P(None, None, "chan", "tm"),
        check_vma=False,
    )
```

```python
import functools
import math

import jax
import jax.numpy as jnp
from jax import lax
from jax.experimental import pallas as pl
from jax.experimental.pallas import tpu as pltpu
from jax.sharding import PartitionSpec as P

VS = 8
STEPS = 2
LAGS = 1024
TAPS = 32
LANES = 128
FINE = 16


def body(C, T, rows, taps_hbm, pair_hbm, blocks_hbm, rec_hbm, out_ref,
         taps_ref, pair_ref, blocks_ref, rec_ref, local_s,
         halo, filt, pfilt, pw, chw, tw, ts, wp, wall,
         halo_s, halo_r, part_s, part_r, pw_s, pw_r, ch_s, ch_r, tw_s, tw_r, ts_s, ts_r):
    me = lax.axis_index("chan")
    t = lax.axis_index("tm")
    f32, bf16 = jnp.float32, jnp.bfloat16
    samples = rec_ref.shape[1] // 4
    lag_dev = LAGS // T
    P_ = max(1, lag_dev // LANES)
    A_ = min(lag_dev, LANES) // FINE
    window = samples * T

    def at_chan(d):
        return lax.rem(me + d, C)

    def at_tm(d):
        return lax.rem(t + d, T)

    loads = [pltpu.make_async_copy(src, dst, local_s.at[i]) for i, (src, dst) in enumerate((
        (taps_hbm, taps_ref), (rec_hbm, rec_ref), (pair_hbm, pair_ref), (blocks_hbm, blocks_ref)))]
    for load in loads:
        load.start()
    barrier = pltpu.get_barrier_semaphore()
    for d in range(1, C):
        pl.semaphore_signal(barrier, inc=1, device_id={"chan": at_chan(d)}, device_id_type=pl.DeviceIdType.MESH)
    for d in range(1, T):
        pl.semaphore_signal(barrier, inc=1, device_id={"tm": at_tm(d)}, device_id_type=pl.DeviceIdType.MESH)

    def remote(src, dst, ssem, rsem, where):
        return pltpu.make_async_remote_copy(
            src_ref=src, dst_ref=dst, send_sem=ssem, recv_sem=rsem,
            device_id=where, device_id_type=pl.DeviceIdType.MESH)

    group = 4 * LANES
    depth = LANES + group
    j = lax.broadcasted_iota(jnp.int32, (depth, LANES), 0)
    n = lax.broadcasted_iota(jnp.int32, (depth, LANES), 1)
    tap = 4 * n + 3 - (j - LANES)
    band = jnp.zeros((depth, LANES), f32)
    loads[0].wait()
    for k in range(TAPS):
        band = jnp.where(tap == k, taps_ref[k], band)
    hi = band.astype(bf16)
    lo = (band - hi.astype(f32)).astype(bf16)
    band2 = jnp.concatenate([hi, lo], axis=1)

    for load in loads[1:]:
        load.wait()
    pl.semaphore_wait(barrier, C + T - 2)
    tail = rec_ref.shape[1] - LANES
    halo_copy = remote(rec_ref.at[:, pl.ds(tail, LANES)], halo, halo_s, halo_r, {"tm": at_tm(1)})
    halo_copy.start()

    wp[:, window:] = jnp.zeros((rows, wp.shape[1] - window), f32)

    groups = samples // LANES
    parts = []
    for g in range(groups):
        if g == 0:
            first = jnp.zeros((rows, LANES), bf16)
        else:
            first = rec_ref[:, group * g - LANES:group * g]
        parts.append(jnp.concatenate([first, rec_ref[:, group * g:group * (g + 1)]], axis=1))
    lhs = jnp.concatenate(parts, axis=0)
    both = jnp.dot(lhs, band2, preferred_element_type=f32)
    res = both[:, :LANES] + both[:, LANES:]
    halo_copy.wait()
    edge = jnp.dot(halo[...], band2[:LANES], preferred_element_type=f32)
    edge = edge[:, :LANES] + edge[:, LANES:]
    edge = jnp.where(t > 0, edge, jnp.zeros_like(edge))
    for g in range(groups):
        piece = res[rows * g:rows * (g + 1)]
        if g == 0:
            piece = piece + edge
        filt[:, LANES * g:LANES * (g + 1)] = piece
    part_copy = remote(filt, pfilt, part_s, part_r, {"chan": at_chan(C // 2)})
    part_copy.start()
    rr = lax.broadcasted_iota(jnp.int32, (rows, rows), 0)
    cc = lax.broadcasted_iota(jnp.int32, (rows, rows), 1)
    pick = jnp.zeros((rows, rows), jnp.int32)
    for r in range(rows):
        pick = jnp.where(rr == r, pair_ref[0, r], pick)
    perm = jnp.where(pick == cc, 1.0, 0.0).astype(f32)
    part_copy.wait()
    filtered = 0.5 * (filt[...] + jnp.dot(perm, pfilt[...], precision=lax.Precision.HIGHEST,
                                          preferred_element_type=f32))
    sq = filtered * filtered
    acc = sq[:, :LANES]
    for g in range(1, groups):
        acc = acc + sq[:, LANES * g:LANES * (g + 1)]
    pw[t] = acc

    def spread(buf, slot, ssem, rsem, count, axis, place):
        sends = [remote(buf.at[slot], buf.at[slot], ssem.at[d], rsem.at[d], {axis: place(d)})
                 for d in range(1, count)]
        for s in sends:
            s.start()
        return sends

    def arrive(buf, ssem, rsem, count, axis, place):
        for d in range(1, count):
            slot = place(count - d)
            remote(buf.at[slot], buf.at[slot], ssem.at[d], rsem.at[d], {axis: place(d)}).wait_recv()

    pw_sends = spread(pw, t, pw_s, pw_r, T, "tm", at_tm)
    arrive(pw, pw_s, pw_r, T, "tm", at_tm)
    total = pw[0]
    for i in range(1, T):
        total = total + pw[i]
    power = jnp.sum(total, axis=1, keepdims=True) / window
    white = (filtered * lax.rsqrt(power + 1e-6)).astype(bf16)
    chw[me] = white
    tw[t] = white
    ch_sends = spread(chw, me, ch_s, ch_r, C, "chan", at_chan)
    tw_sends = spread(tw, t, tw_s, tw_r, T, "tm", at_tm)

    arrive(chw, ch_s, ch_r, C, "chan", at_chan)
    picked = []
    per = rows // VS
    for step in range(STEPS):
        blk = blocks_ref[step]
        owner = lax.div(blk, per)
        within = lax.rem(blk, per)
        x = chw[owner].astype(f32)
        half = x[:VS]
        for q in range(1, per):
            half = jnp.where(within == q, x[VS * q:VS * (q + 1)], half)
        picked.append(half)
    ts[t] = jnp.concatenate(picked, axis=0).astype(bf16)
    ts_sends = spread(ts, t, ts_s, ts_r, T, "tm", at_tm)
    arrive(tw, tw_s, tw_r, T, "tm", at_tm)
    for i in range(T):
        wp[:, samples * i:samples * (i + 1)] = tw[i].astype(f32)

    lag0 = t * lag_dev
    wide = samples + LANES * P_
    if lag_dev % LANES == 0:
        base, rest = lag0, 0
    else:
        base = lax.div(lag0, LANES) * LANES
        rest = lax.rem(lag0, LANES)

    for i in range(T):
        wrows = wp[:, pl.ds(pl.multiple_of(i * samples + base, LANES), wide)]
        for a in range(A_):
            rolled = wrows
            if lag_dev % LANES:
                rolled = pltpu.roll(wrows, wide - FINE * a - rest, 1)
            elif a:
                rolled = pltpu.roll(wrows, wide - FINE * a, 1)
            for p in range(P_):
                r0 = (p * A_ + a) * rows
                wall[r0:r0 + rows, samples * i:samples * (i + 1)] = (
                    rolled[:, LANES * p:LANES * p + samples].astype(bf16))
    wall[:, window:] = jnp.zeros((wall.shape[0], LANES), bf16)

    span = samples + LANES

    def term(slot):
        srows = jnp.concatenate([ts[slot].astype(f32), jnp.zeros((rows, LANES), f32)], axis=1)
        xs = []
        for s in range(STEPS * VS):
            one = jnp.broadcast_to(srows[s:s + 1], (FINE, span))
            xs.append(pltpu.roll(one, 0, 1, stride=1, stride_axis=0).astype(bf16))
        ws = wall[:, pl.ds(pl.multiple_of(slot * samples, LANES), span)]
        return lax.dot_general(ws, jnp.concatenate(xs, axis=0),
                               (((1,), (1,)), ((), ())), preferred_element_type=f32)

    z = term(t)
    for d in range(1, T):
        slot = at_tm(T - d)
        remote(ts.at[slot], ts.at[slot], ts_s.at[d], ts_r.at[d], {"tm": at_tm(d)}).wait_recv()
        z = z + term(slot)
    z = z * (1.0 / math.sqrt(window))

    lane_group = lax.broadcasted_iota(jnp.int32, (rows, LANES), 1) // FINE
    per_tile = LANES // FINE
    width = min(lag_dev, LANES)
    for p in range(P_):
        for s in range(STEPS * VS):
            lo_s = s // per_tile * LANES
            o = None
            for a in range(A_):
                r0 = (p * A_ + a) * rows
                tile = z[r0:r0 + rows, lo_s:lo_s + LANES]
                sh = (FINE * (a - s % per_tile)) % LANES
                if sh:
                    tile = pltpu.roll(tile, sh, 1)
                o = tile if o is None else jnp.where(lane_group == a, tile, o)
            out_ref[s, :, LANES * p:LANES * p + width] = o[:, :width]

    for s in pw_sends + ch_sends + tw_sends + ts_sends:
        s.wait_send()


def shards(records, pair_rows, fir_taps, source_blocks):
    C = lax.axis_size("chan")
    T = lax.axis_size("tm")
    rows, raw = records.shape
    samples = raw // 4
    f32, bf16 = jnp.float32, jnp.bfloat16
    dma = pltpu.SemaphoreType.DMA
    vmem = pl.BlockSpec(memory_space=pltpu.VMEM)
    hbm = pl.BlockSpec(memory_space=pltpu.HBM)
    out = pl.pallas_call(
        functools.partial(body, C, T, rows),
        out_shape=jax.ShapeDtypeStruct((STEPS * VS, rows, LAGS // T), f32),
        in_specs=[hbm] * 4,
        out_specs=vmem,
        scratch_shapes=[
            pltpu.SMEM(fir_taps.shape, f32),
            pltpu.SMEM(pair_rows.shape, jnp.int32),
            pltpu.SMEM(source_blocks.shape, jnp.int32),
            pltpu.VMEM(records.shape, bf16),
            dma((4,)),
            pltpu.VMEM((rows, LANES), bf16),
            pltpu.VMEM((rows, samples), f32),
            pltpu.VMEM((rows, samples), f32),
            pltpu.VMEM((T, rows, LANES), f32),
            pltpu.VMEM((C, rows, samples), bf16),
            pltpu.VMEM((T, rows, samples), bf16),
            pltpu.VMEM((T, rows, samples), bf16),
            pltpu.VMEM((rows, T * samples + LAGS + LANES), f32),
            pltpu.VMEM((LAGS // T // FINE * rows, T * samples + LANES), bf16),
            dma, dma, dma, dma,
            dma((T,)), dma((T,)), dma((C,)), dma((C,)),
            dma((T,)), dma((T,)), dma((T,)), dma((T,)),
        ],
        compiler_params=pltpu.CompilerParams(
            collective_id=0, has_side_effects=True, vmem_limit_bytes=60 * 2**20),
        cost_estimate=pl.CostEstimate(flops=600_000_000, bytes_accessed=1_000_000, transcendentals=0),
    )(fir_taps, pair_rows, source_blocks, records)
    return out.reshape(STEPS, VS, rows, LAGS // T)


def solution(mesh):
    return jax.shard_map(
        shards,
        mesh=mesh,
        in_specs=(P("chan", "tm"), P("chan", None), P(), P()),
        out_specs=P(None, None, "chan", "tm"),
        check_vma=False,
    )
```

```python
import functools
import math

import jax
import jax.numpy as jnp
from jax import lax
from jax.experimental import pallas as pl
from jax.experimental.pallas import tpu as pltpu
from jax.sharding import PartitionSpec as P

VS = 8
STEPS = 2
LAGS = 1024
TAPS = 32
LANES = 128
FINE = 16


def body(C, T, rows, taps_hbm, pair_hbm, blocks_hbm, rec_hbm, out_ref,
         taps_ref, pair_ref, blocks_ref, rec_ref, local_s,
         halo, phalo, praw, pw, chw, tw, ts, wp, wall,
         halo_s, halo_r, phalo_s, phalo_r, part_s, part_r, pw_s, pw_r, ch_s, ch_r, tw_s, tw_r, ts_s, ts_r):
    me = lax.axis_index("chan")
    t = lax.axis_index("tm")
    f32, bf16 = jnp.float32, jnp.bfloat16
    samples = rec_ref.shape[1] // 4
    lag_dev = LAGS // T
    P_ = max(1, lag_dev // LANES)
    A_ = min(lag_dev, LANES) // FINE
    window = samples * T

    def at_chan(d):
        return lax.rem(me + d, C)

    def at_tm(d):
        return lax.rem(t + d, T)

    loads = [pltpu.make_async_copy(src, dst, local_s.at[i]) for i, (src, dst) in enumerate((
        (taps_hbm, taps_ref), (rec_hbm, rec_ref), (pair_hbm, pair_ref), (blocks_hbm, blocks_ref)))]
    for load in loads:
        load.start()
    barrier = pltpu.get_barrier_semaphore()
    for d in range(1, C):
        pl.semaphore_signal(barrier, inc=1, device_id={"chan": at_chan(d)}, device_id_type=pl.DeviceIdType.MESH)
    for d in range(1, T):
        pl.semaphore_signal(barrier, inc=1, device_id={"tm": at_tm(d)}, device_id_type=pl.DeviceIdType.MESH)

    pl.semaphore_signal(barrier, inc=1, device_id={"chan": at_chan(C // 2), "tm": at_tm(T - 1)},
                        device_id_type=pl.DeviceIdType.MESH)

    def remote(src, dst, ssem, rsem, where):
        return pltpu.make_async_remote_copy(
            src_ref=src, dst_ref=dst, send_sem=ssem, recv_sem=rsem,
            device_id=where, device_id_type=pl.DeviceIdType.MESH)

    group = 4 * LANES
    depth = LANES + group
    j = lax.broadcasted_iota(jnp.int32, (depth, LANES), 0)
    n = lax.broadcasted_iota(jnp.int32, (depth, LANES), 1)
    tap = 4 * n + 3 - (j - LANES)
    band = jnp.zeros((depth, LANES), f32)
    loads[0].wait()
    for k in range(TAPS):
        band = jnp.where(tap == k, taps_ref[k], band)
    hi = band.astype(bf16)
    lo = (band - hi.astype(f32)).astype(bf16)
    band2 = jnp.concatenate([hi, lo], axis=1)

    for load in loads[1:]:
        load.wait()
    pl.semaphore_wait(barrier, C + T - 1)
    tail = rec_ref.shape[1] - LANES
    last = rec_ref.at[:, pl.ds(tail, LANES)]
    phalo_copy = remote(last, phalo, phalo_s, phalo_r, {"chan": at_chan(C // 2), "tm": at_tm(1)})
    halo_copy = remote(last, halo, halo_s, halo_r, {"tm": at_tm(1)})
    part_copy = remote(rec_ref, praw, part_s, part_r, {"chan": at_chan(C // 2)})
    phalo_copy.start()
    halo_copy.start()
    part_copy.start()

    wp[:, window:] = jnp.zeros((rows, wp.shape[1] - window), f32)
    wall[:, window:] = jnp.zeros((wall.shape[0], LANES), bf16)
    rr = lax.broadcasted_iota(jnp.int32, (rows, rows), 0)
    cc = lax.broadcasted_iota(jnp.int32, (rows, rows), 1)
    pick = jnp.zeros((rows, rows), jnp.int32)
    for r in range(rows):
        pick = jnp.where(rr == r, pair_ref[0, r], pick)
    perm = jnp.where(pick == cc, 1.0, 0.0).astype(bf16)

    groups = samples // LANES

    def filter_rows(raw):
        parts = []
        for g in range(groups):
            if g == 0:
                first = jnp.zeros((rows, LANES), bf16)
            else:
                first = raw[:, group * g - LANES:group * g]
            parts.append(jnp.concatenate([first, raw[:, group * g:group * (g + 1)]], axis=1))
        both = jnp.dot(jnp.concatenate(parts, axis=0), band2, preferred_element_type=f32)
        return both[:, :LANES] + both[:, LANES:]

    def permuted(x):
        return jnp.dot(perm, x, preferred_element_type=f32).astype(bf16)

    own = filter_rows(rec_ref[...])
    phalo_copy.wait()
    halo_copy.wait()
    edges = jnp.concatenate([halo[...], permuted(phalo[...])], axis=0)
    edges = jnp.dot(edges, band2[:LANES], preferred_element_type=f32)
    edges = edges[:, :LANES] + edges[:, LANES:]
    edge = edges[:rows] + edges[rows:]
    edge = jnp.where(t > 0, edge, jnp.zeros_like(edge))
    part_copy.wait()
    res = own + filter_rows(permuted(praw[...]))
    filtered = 0.5 * jnp.concatenate(
        [res[:rows] + edge] + [res[rows * g:rows * (g + 1)] for g in range(1, groups)], axis=1)
    sq = filtered * filtered
    acc = sq[:, :LANES]
    for g in range(1, groups):
        acc = acc + sq[:, LANES * g:LANES * (g + 1)]
    pw[t] = acc

    def spread(buf, slot, ssem, rsem, count, axis, place):
        sends = [remote(buf.at[slot], buf.at[slot], ssem.at[d], rsem.at[d], {axis: place(d)})
                 for d in range(1, count)]
        for s in sends:
            s.start()
        return sends

    def arrive(buf, ssem, rsem, count, axis, place):
        for d in range(1, count):
            slot = place(count - d)
            remote(buf.at[slot], buf.at[slot], ssem.at[d], rsem.at[d], {axis: place(d)}).wait_recv()

    pw_sends = spread(pw, t, pw_s, pw_r, T, "tm", at_tm)
    arrive(pw, pw_s, pw_r, T, "tm", at_tm)
    total = pw[0]
    for i in range(1, T):
        total = total + pw[i]
    power = jnp.sum(total, axis=1, keepdims=True) / window
    white = (filtered * lax.rsqrt(power + 1e-6)).astype(bf16)
    chw[me] = white
    tw[t] = white
    ch_sends = spread(chw, me, ch_s, ch_r, C, "chan", at_chan)
    tw_sends = spread(tw, t, tw_s, tw_r, T, "tm", at_tm)

    arrive(chw, ch_s, ch_r, C, "chan", at_chan)
    picked = []
    per = rows // VS
    for step in range(STEPS):
        blk = blocks_ref[step]
        owner = lax.div(blk, per)
        within = lax.rem(blk, per)
        x = chw[owner].astype(f32)
        half = x[:VS]
        for q in range(1, per):
            half = jnp.where(within == q, x[VS * q:VS * (q + 1)], half)
        picked.append(half)
    ts[t] = jnp.concatenate(picked, axis=0).astype(bf16)
    ts_sends = spread(ts, t, ts_s, ts_r, T, "tm", at_tm)
    arrive(tw, tw_s, tw_r, T, "tm", at_tm)
    for i in range(T):
        wp[:, samples * i:samples * (i + 1)] = tw[i].astype(f32)

    lag0 = t * lag_dev
    wide = samples + LANES * P_
    if lag_dev % LANES == 0:
        base, rest = lag0, 0
    else:
        base = lax.div(lag0, LANES) * LANES
        rest = lax.rem(lag0, LANES)

    for i in range(T):
        wrows = wp[:, pl.ds(pl.multiple_of(i * samples + base, LANES), wide)]
        for a in range(A_):
            rolled = wrows
            if lag_dev % LANES:
                rolled = pltpu.roll(wrows, wide - FINE * a - rest, 1)
            elif a:
                rolled = pltpu.roll(wrows, wide - FINE * a, 1)
            for p in range(P_):
                r0 = (p * A_ + a) * rows
                wall[r0:r0 + rows, samples * i:samples * (i + 1)] = (
                    rolled[:, LANES * p:LANES * p + samples].astype(bf16))

    span = samples + LANES

    def term(slot):
        srows = jnp.concatenate([ts[slot].astype(f32), jnp.zeros((rows, LANES), f32)], axis=1)
        xs = []
        for s in range(STEPS * VS):
            one = jnp.broadcast_to(srows[s:s + 1], (FINE, span))
            xs.append(pltpu.roll(one, 0, 1, stride=1, stride_axis=0).astype(bf16))
        ws = wall[:, pl.ds(pl.multiple_of(slot * samples, LANES), span)]
        return lax.dot_general(ws, jnp.concatenate(xs, axis=0),
                               (((1,), (1,)), ((), ())), preferred_element_type=f32)

    z = term(t)
    for d in range(1, T):
        slot = at_tm(T - d)
        remote(ts.at[slot], ts.at[slot], ts_s.at[d], ts_r.at[d], {"tm": at_tm(d)}).wait_recv()
        z = z + term(slot)
    z = z * (1.0 / math.sqrt(window))

    lane_group = lax.broadcasted_iota(jnp.int32, (rows, LANES), 1) // FINE
    per_tile = LANES // FINE
    width = min(lag_dev, LANES)
    for p in range(P_):
        for lo_s in range(0, STEPS * VS, per_tile):
            turned = []
            for a in range(A_):
                r0 = (p * A_ + a) * rows
                tile = z[r0:r0 + rows, lo_s * FINE:lo_s * FINE + LANES]
                turned.append(pltpu.roll(tile, FINE * a, 1) if a else tile)
            for s in range(per_tile):
                o = turned[0]
                for a in range(1, A_):
                    o = jnp.where(lane_group == (s + a) % per_tile, turned[a], o)
                if s:
                    o = pltpu.roll(o, LANES - FINE * s, 1)
                out_ref[lo_s + s, :, LANES * p:LANES * p + width] = o[:, :width]

    for s in pw_sends + ch_sends + tw_sends + ts_sends:
        s.wait_send()


def shards(records, pair_rows, fir_taps, source_blocks):
    C = lax.axis_size("chan")
    T = lax.axis_size("tm")
    rows, raw = records.shape
    samples = raw // 4
    f32, bf16 = jnp.float32, jnp.bfloat16
    dma = pltpu.SemaphoreType.DMA
    vmem = pl.BlockSpec(memory_space=pltpu.VMEM)
    hbm = pl.BlockSpec(memory_space=pltpu.HBM)
    out = pl.pallas_call(
        functools.partial(body, C, T, rows),
        out_shape=jax.ShapeDtypeStruct((STEPS * VS, rows, LAGS // T), f32),
        in_specs=[hbm] * 4,
        out_specs=vmem,
        scratch_shapes=[
            pltpu.SMEM(fir_taps.shape, f32),
            pltpu.SMEM(pair_rows.shape, jnp.int32),
            pltpu.SMEM(source_blocks.shape, jnp.int32),
            pltpu.VMEM(records.shape, bf16),
            dma((4,)),
            pltpu.VMEM((rows, LANES), bf16),
            pltpu.VMEM((rows, LANES), bf16),
            pltpu.VMEM((rows, raw), bf16),
            pltpu.VMEM((T, rows, LANES), f32),
            pltpu.VMEM((C, rows, samples), bf16),
            pltpu.VMEM((T, rows, samples), bf16),
            pltpu.VMEM((T, rows, samples), bf16),
            pltpu.VMEM((rows, T * samples + LAGS + LANES), f32),
            pltpu.VMEM((LAGS // T // FINE * rows, T * samples + LANES), bf16),
            dma, dma, dma, dma, dma, dma,
            dma((T,)), dma((T,)), dma((C,)), dma((C,)),
            dma((T,)), dma((T,)), dma((T,)), dma((T,)),
        ],
        compiler_params=pltpu.CompilerParams(
            collective_id=0, has_side_effects=True, vmem_limit_bytes=60 * 2**20),
        cost_estimate=pl.CostEstimate(flops=600_000_000, bytes_accessed=1_000_000, transcendentals=0),
    )(fir_taps, pair_rows, source_blocks, records)
    return out.reshape(STEPS, VS, rows, LAGS // T)


def solution(mesh):
    return jax.shard_map(
        shards,
        mesh=mesh,
        in_specs=(P("chan", "tm"), P("chan", None), P(), P()),
        out_specs=P(None, None, "chan", "tm"),
        check_vma=False,
    )
```

```python
import functools
import math

import jax
import jax.numpy as jnp
from jax import lax
from jax.experimental import pallas as pl
from jax.experimental.pallas import tpu as pltpu
from jax.sharding import PartitionSpec as P

VS = 8
STEPS = 2
LAGS = 1024
TAPS = 32
LANES = 128
FINE = 16


def body(C, T, rows, taps_hbm, pair_hbm, blocks_hbm, rec_hbm, out_ref,
         taps_ref, pair_ref, blocks_ref, rec_ref, local_s,
         halo, phalo, praw, pw, chw, tw, ts, wp, wall,
         halo_s, halo_r, phalo_s, phalo_r, part_s, part_r, pw_s, pw_r, ch_s, ch_r, tw_s, tw_r, ts_s, ts_r):
    me = lax.axis_index("chan")
    t = lax.axis_index("tm")
    f32, bf16 = jnp.float32, jnp.bfloat16
    samples = rec_ref.shape[1] // 4
    lag_dev = LAGS // T
    P_ = max(1, lag_dev // LANES)
    A_ = min(lag_dev, LANES) // FINE
    window = samples * T

    def at_chan(d):
        return lax.rem(me + d, C)

    def at_tm(d):
        return lax.rem(t + d, T)

    loads = [pltpu.make_async_copy(src, dst, local_s.at[i]) for i, (src, dst) in enumerate((
        (taps_hbm, taps_ref), (rec_hbm, rec_ref), (pair_hbm, pair_ref), (blocks_hbm, blocks_ref)))]
    for load in loads:
        load.start()
    barrier = pltpu.get_barrier_semaphore()
    for d in range(1, C):
        pl.semaphore_signal(barrier, inc=1, device_id={"chan": at_chan(d)}, device_id_type=pl.DeviceIdType.MESH)
    for d in range(1, T):
        pl.semaphore_signal(barrier, inc=1, device_id={"tm": at_tm(d)}, device_id_type=pl.DeviceIdType.MESH)

    pl.semaphore_signal(barrier, inc=1, device_id={"chan": at_chan(C // 2), "tm": at_tm(T - 1)},
                        device_id_type=pl.DeviceIdType.MESH)

    def remote(src, dst, ssem, rsem, where):
        return pltpu.make_async_remote_copy(
            src_ref=src, dst_ref=dst, send_sem=ssem, recv_sem=rsem,
            device_id=where, device_id_type=pl.DeviceIdType.MESH)

    group = 4 * LANES
    depth = LANES + group
    j = lax.broadcasted_iota(jnp.int32, (depth, LANES), 0)
    n = lax.broadcasted_iota(jnp.int32, (depth, LANES), 1)
    tap = 4 * n + 3 - (j - LANES)
    band = jnp.zeros((depth, LANES), f32)
    loads[0].wait()
    for k in range(TAPS):
        band = jnp.where(tap == k, taps_ref[k], band)
    hi = band.astype(bf16)
    lo = (band - hi.astype(f32)).astype(bf16)
    band2 = jnp.concatenate([hi, lo], axis=1)

    for load in loads[1:]:
        load.wait()
    pl.semaphore_wait(barrier, C + T - 1)
    tail = rec_ref.shape[1] - LANES
    last = rec_ref.at[:, pl.ds(tail, LANES)]
    phalo_copy = remote(last, phalo, phalo_s, phalo_r, {"chan": at_chan(C // 2), "tm": at_tm(1)})
    halo_copy = remote(last, halo, halo_s, halo_r, {"tm": at_tm(1)})
    part_copy = remote(rec_ref, praw, part_s, part_r, {"chan": at_chan(C // 2)})
    phalo_copy.start()
    halo_copy.start()
    part_copy.start()

    wp[:, window:] = jnp.zeros((rows, wp.shape[1] - window), f32)
    wall[:, window:] = jnp.zeros((wall.shape[0], LANES), bf16)
    rr = lax.broadcasted_iota(jnp.int32, (rows, rows), 0)
    cc = lax.broadcasted_iota(jnp.int32, (rows, rows), 1)
    pick = jnp.zeros((rows, rows), jnp.int32)
    for r in range(rows):
        pick = jnp.where(rr == r, pair_ref[0, r], pick)
    perm = jnp.where(pick == cc, 1.0, 0.0).astype(bf16)

    groups = samples // LANES

    def filter_rows(raw):
        parts = []
        for g in range(groups):
            if g == 0:
                first = jnp.zeros((rows, LANES), bf16)
            else:
                first = raw[:, group * g - LANES:group * g]
            parts.append(jnp.concatenate([first, raw[:, group * g:group * (g + 1)]], axis=1))
        both = jnp.dot(jnp.concatenate(parts, axis=0), band2, preferred_element_type=f32)
        return both[:, :LANES] + both[:, LANES:]

    def permuted(x):
        return jnp.dot(perm, x, preferred_element_type=f32).astype(bf16)

    own = filter_rows(rec_ref[...])
    phalo_copy.wait()
    halo_copy.wait()
    edges = jnp.concatenate([halo[...], permuted(phalo[...])], axis=0)
    edges = jnp.dot(edges, band2[:LANES], preferred_element_type=f32)
    edges = edges[:, :LANES] + edges[:, LANES:]
    edge = edges[:rows] + edges[rows:]
    edge = jnp.where(t > 0, edge, jnp.zeros_like(edge))
    part_copy.wait()
    res = own + filter_rows(permuted(praw[...]))
    filtered = 0.5 * jnp.concatenate(
        [res[:rows] + edge] + [res[rows * g:rows * (g + 1)] for g in range(1, groups)], axis=1)
    sq = filtered * filtered
    acc = sq[:, :LANES]
    for g in range(1, groups):
        acc = acc + sq[:, LANES * g:LANES * (g + 1)]
    pw[t] = acc

    def spread(buf, slot, ssem, rsem, count, axis, place):
        sends = [remote(buf.at[slot], buf.at[slot], ssem.at[d], rsem.at[d], {axis: place(d)})
                 for d in range(1, count)]
        for s in sends:
            s.start()
        return sends

    def arrive(buf, ssem, rsem, count, axis, place):
        for d in range(1, count):
            slot = place(count - d)
            remote(buf.at[slot], buf.at[slot], ssem.at[d], rsem.at[d], {axis: place(d)}).wait_recv()

    pw_sends = spread(pw, t, pw_s, pw_r, T, "tm", at_tm)
    arrive(pw, pw_s, pw_r, T, "tm", at_tm)
    total = pw[0]
    for i in range(1, T):
        total = total + pw[i]
    power = jnp.sum(total, axis=1, keepdims=True) / window
    white = (filtered * lax.rsqrt(power + 1e-6)).astype(bf16)
    chw[me] = white
    tw[t] = white
    ch_sends = spread(chw, me, ch_s, ch_r, C, "chan", at_chan)
    tw_sends = spread(tw, t, tw_s, tw_r, T, "tm", at_tm)

    arrive(chw, ch_s, ch_r, C, "chan", at_chan)
    picked = []
    per = rows // VS
    for step in range(STEPS):
        blk = blocks_ref[step]
        owner = lax.div(blk, per)
        within = lax.rem(blk, per)
        x = chw[owner].astype(f32)
        half = x[:VS]
        for q in range(1, per):
            half = jnp.where(within == q, x[VS * q:VS * (q + 1)], half)
        picked.append(half)
    ts[t] = jnp.concatenate(picked, axis=0).astype(bf16)
    ts_sends = spread(ts, t, ts_s, ts_r, T, "tm", at_tm)
    arrive(tw, tw_s, tw_r, T, "tm", at_tm)
    for i in range(T):
        wp[:, samples * i:samples * (i + 1)] = tw[i].astype(f32)

    lag0 = t * lag_dev
    wide = samples + LANES * P_
    if lag_dev % LANES == 0:
        base, rest = lag0, 0
    else:
        base = lax.div(lag0, LANES) * LANES
        rest = lax.rem(lag0, LANES)

    for i in range(T):
        wrows = wp[:, pl.ds(pl.multiple_of(i * samples + base, LANES), wide)]
        for a in range(A_):
            rolled = wrows
            if lag_dev % LANES:
                rolled = pltpu.roll(wrows, wide - FINE * a - rest, 1)
            elif a:
                rolled = pltpu.roll(wrows, wide - FINE * a, 1)
            for p in range(P_):
                r0 = (p * A_ + a) * rows
                wall[r0:r0 + rows, samples * i:samples * (i + 1)] = (
                    rolled[:, LANES * p:LANES * p + samples].astype(bf16))

    span = samples + LANES

    def term(slot):
        srows = jnp.concatenate([ts[slot].astype(f32), jnp.zeros((rows, LANES), f32)], axis=1)
        xs = []
        for s in range(STEPS * VS):
            one = jnp.broadcast_to(srows[s:s + 1], (FINE, span))
            xs.append(pltpu.roll(one, 0, 1, stride=1, stride_axis=0).astype(bf16))
        ws = wall[:, pl.ds(pl.multiple_of(slot * samples, LANES), span)]
        return lax.dot_general(ws, jnp.concatenate(xs, axis=0),
                               (((1,), (1,)), ((), ())), preferred_element_type=f32)

    z = term(t)
    low = t < T // 2
    edge_dist = jnp.where(low, t, T - 1 - t)
    for k in range(T - 1):
        up = jnp.where(k >= edge_dist, k + 1, k)
        slot = jnp.where(low, up, T - 1 - up)
        d = lax.rem(t - slot + T, T)
        remote(ts.at[slot], ts.at[slot], ts_s.at[d], ts_r.at[d], {"tm": at_tm(d)}).wait_recv()
        z = z + term(slot)
    z = z * (1.0 / math.sqrt(window))

    lane_group = lax.broadcasted_iota(jnp.int32, (rows, LANES), 1) // FINE
    per_tile = LANES // FINE
    width = min(lag_dev, LANES)
    for p in range(P_):
        for lo_s in range(0, STEPS * VS, per_tile):
            turned = []
            for a in range(A_):
                r0 = (p * A_ + a) * rows
                tile = z[r0:r0 + rows, lo_s * FINE:lo_s * FINE + LANES]
                turned.append(pltpu.roll(tile, FINE * a, 1) if a else tile)
            for s in range(per_tile):
                o = turned[0]
                for a in range(1, A_):
                    o = jnp.where(lane_group == (s + a) % per_tile, turned[a], o)
                if s:
                    o = pltpu.roll(o, LANES - FINE * s, 1)
                out_ref[lo_s + s, :, LANES * p:LANES * p + width] = o[:, :width]

    for s in pw_sends + ch_sends + tw_sends + ts_sends:
        s.wait_send()


def shards(records, pair_rows, fir_taps, source_blocks):
    C = lax.axis_size("chan")
    T = lax.axis_size("tm")
    rows, raw = records.shape
    samples = raw // 4
    f32, bf16 = jnp.float32, jnp.bfloat16
    dma = pltpu.SemaphoreType.DMA
    vmem = pl.BlockSpec(memory_space=pltpu.VMEM)
    hbm = pl.BlockSpec(memory_space=pltpu.HBM)
    out = pl.pallas_call(
        functools.partial(body, C, T, rows),
        out_shape=jax.ShapeDtypeStruct((STEPS * VS, rows, LAGS // T), f32),
        in_specs=[hbm] * 4,
        out_specs=vmem,
        scratch_shapes=[
            pltpu.SMEM(fir_taps.shape, f32),
            pltpu.SMEM(pair_rows.shape, jnp.int32),
            pltpu.SMEM(source_blocks.shape, jnp.int32),
            pltpu.VMEM(records.shape, bf16),
            dma((4,)),
            pltpu.VMEM((rows, LANES), bf16),
            pltpu.VMEM((rows, LANES), bf16),
            pltpu.VMEM((rows, raw), bf16),
            pltpu.VMEM((T, rows, LANES), f32),
            pltpu.VMEM((C, rows, samples), bf16),
            pltpu.VMEM((T, rows, samples), bf16),
            pltpu.VMEM((T, rows, samples), bf16),
            pltpu.VMEM((rows, T * samples + LAGS + LANES), f32),
            pltpu.VMEM((LAGS // T // FINE * rows, T * samples + LANES), bf16),
            dma, dma, dma, dma, dma, dma,
            dma((T,)), dma((T,)), dma((C,)), dma((C,)),
            dma((T,)), dma((T,)), dma((T,)), dma((T,)),
        ],
        compiler_params=pltpu.CompilerParams(
            collective_id=0, has_side_effects=True, vmem_limit_bytes=60 * 2**20),
        cost_estimate=pl.CostEstimate(flops=600_000_000, bytes_accessed=1_000_000, transcendentals=0),
    )(fir_taps, pair_rows, source_blocks, records)
    return out.reshape(STEPS, VS, rows, LAGS // T)


def solution(mesh):
    return jax.shard_map(
        shards,
        mesh=mesh,
        in_specs=(P("chan", "tm"), P("chan", None), P(), P()),
        out_specs=P(None, None, "chan", "tm"),
        check_vma=False,
    )
```
